256 devices in a mesh: ab: 16 (over y, x_lo, core), cd: 16 (over z, x_hi).
Axes of the slice: x: 4 (x_hi: 2, x_lo: 2; x = x_hi * 2 + x_lo), y: 4, z: 8, core: 2. Of those that a mesh axis runs over, the one named last changes fastest.
Arguments:
- amplitudes: bfloat16 [128, 32768], P('ab', 'cd'), may hold values from -6 to 6
- integrals: bfloat16 [32768, 32768], P('ab', 'cd'), as said below
- vir_energy: float32 [32768], replicated, may hold values from 0.6 to 1.6
- occ_energy: float32 [128], replicated, may hold values from -0.5 to -0.1
Outputs:
- ladder_one: bfloat16 [128, 32768], P('cd', 'ab')
- ladder_two: bfloat16 [128, 32768], P('ab', 'cd')
- ladder_three: bfloat16 [128, 32768], P('cd', 'ab')
The draws below stay inside these ranges and needn't reach their ends.
Inputs may be any that keep to these rules, and one draw needn't show every extreme that they name: integrals is symmetric: integrals[x, y] equals integrals[y, x].
All inputs are finite; a program needn't handle non-finite values.
Results may differ from the reference program's by a relative error of at most 0.02.
Values may be sent and summed in bfloat16 or wider, within the bound.
A program may use at most 64 MiB of HBM per device.

```python
import jax
import jax.numpy as jnp
from jax import lax

P_SIZE = 32768
IJ = 128


def draw_integrals(key, part):
    key = jax.random.fold_in(key, 7)
    base = jax.random.normal(key, (P_SIZE, P_SIZE), jnp.float32)
    return ((base + base.T) * 0.5 ** 0.5 * P_SIZE ** (-0.5)).astype(jnp.bfloat16)


def block_levels(rng, shape, pieces, low, top_value):
    def one(dim, parts):
        draws = jax.random.uniform(jax.random.fold_in(jax.random.fold_in(rng, 6), dim), (parts,), jnp.float32, low / len(pieces), top_value / len(pieces))
        return jnp.repeat(jnp.exp(draws), shape[dim] // parts).reshape((-1,) + (1,) * (len(shape) - dim - 1))

    level = one(*pieces[0])
    for cut in pieces[1:]:
        level = level * one(*cut)
    return level


def normal_values(key, extent, spread, most, shards=(), held_as=jnp.bfloat16):
    values = spread * jax.random.normal(key, extent, jnp.float32)
    if shards:
        values = values * block_levels(key, extent, shards, -0.22, 0.18)
    return jnp.clip(values, -most, most).astype(held_as)


def setup_inputs(seed: int = 0) -> dict:
    streams_of = jax.random.split(jax.random.key(seed), 5)
    return {
        "amplitudes": normal_values(streams_of[0], (IJ, P_SIZE), 1.0, 6.0, ((0, 16), (1, 16))),
        "integrals": draw_integrals(jax.random.fold_in(streams_of[4], 71), 0),
        "vir_energy": jnp.clip(jax.random.uniform(streams_of[2], (P_SIZE,), jnp.float32, 0.6, 1.6), 0.6, 1.6),
        "occ_energy": jnp.clip(jax.random.uniform(streams_of[3], (IJ,), jnp.float32, -0.5, -0.1), -0.5, -0.1),
    }


def ladder(amps, integrals):
    return lax.dot_general(amps, integrals, (((1,), (1,)), ((), ())), preferred_element_type=jnp.float32)


def reference(amplitudes, integrals, vir_energy, occ_energy):
    denominator = vir_energy[None, :] - occ_energy[:, None]
    sum_one = ladder(amplitudes, integrals)
    step_one = (sum_one / denominator).astype(jnp.bfloat16)
    sum_two = ladder(step_one, integrals)
    step_two = (sum_two / denominator).astype(jnp.bfloat16)
    sum_three = ladder(step_two, integrals)
    return sum_one.astype(jnp.bfloat16), sum_two.astype(jnp.bfloat16), sum_three.astype(jnp.bfloat16)
```

```python
import functools

import jax
import jax.numpy as jnp
from jax import lax
from jax.experimental import pallas as pl
from jax.experimental.pallas import tpu as pltpu
from jax.sharding import PartitionSpec as P

MESH = pl.DeviceIdType.MESH
F32 = jnp.float32
BF16 = jnp.bfloat16

GROUP = 8
LANES = 128
ROWS = 8
CHUNKS = 4
STAGES = (0, 4, 6, 9, 11)


class Axis:
    def __init__(self, name, other):
        self.name = name
        self.index = lax.axis_index(name)
        self.other = lax.axis_index(other)
        self.group = self.index // 2
        self.pair = self.index % 2

    def device(self, index):
        return (index, self.other) if self.name == "ab" else (self.other, index)

    def peer_group(self, k):
        return (self.group + k) % GROUP

    def source_group(self, k):
        return (self.group + GROUP - k) % GROUP

    def peer(self, k):
        return self.device(self.peer_group(k) * 2 + self.pair)

    def partner(self):
        return self.device(self.group * 2 + 1 - self.pair)


def remote(src, dst, send, recv, device):
    return pltpu.make_async_remote_copy(
        src_ref=src, dst_ref=dst, send_sem=send, recv_sem=recv, device_id=device, device_id_type=MESH
    )


def each_peer(body):
    def step(k, carry):
        body(k)
        return carry

    lax.fori_loop(1, GROUP, step, 0)


def fold(block):
    half = block.shape[1] // 2
    return jnp.concatenate([block[:, :half], block[:, half:]], axis=0)


def unfold(block):
    return jnp.concatenate([block[:ROWS], block[ROWS:]], axis=1)


class Scatter:
    def __init__(self, axis, acc, refs):
        self.axis, self.acc = axis, acc
        self.psnd, self.prcv, self.gsnd, self.grcv, self.pss, self.prs, self.gss, self.grs = refs

    @staticmethod
    def scratch(chunks, width):
        return [
            pltpu.VMEM((chunks, GROUP * ROWS, width), BF16),
            pltpu.VMEM((chunks, GROUP * ROWS, width), BF16),
            pltpu.VMEM((chunks, GROUP, 2 * ROWS, width // 2), BF16),
            pltpu.VMEM((chunks, GROUP, 2 * ROWS, width // 2), BF16),
            pltpu.SemaphoreType.DMA((chunks,)),
            pltpu.SemaphoreType.DMA((chunks,)),
            pltpu.SemaphoreType.DMA((chunks, GROUP)),
            pltpu.SemaphoreType.DMA((chunks, GROUP)),
        ]

    def rows(self, q, g, pair):
        return self.acc[q, pl.ds(pl.multiple_of(g * 16 + pair * ROWS, ROWS), ROWS), :]

    def pair_copy(self, q):
        return remote(
            self.psnd.at[q], self.prcv.at[q], self.pss.at[q], self.prs.at[q], self.axis.partner()
        )

    def group_copy(self, q, k):
        return remote(
            self.gsnd.at[q, self.axis.peer_group(k)],
            self.grcv.at[q, k],
            self.gss.at[q, k],
            self.grs.at[q, k],
            self.axis.peer(k),
        )

    def send_pair(self, q):
        other = 1 - self.axis.pair
        for g in range(0, GROUP, 2):
            two = jnp.concatenate([self.rows(q, g, other), self.rows(q, g + 1, other)], axis=0)
            self.psnd[q, g * ROWS : (g + 2) * ROWS, :] = two.astype(BF16)
        self.pair_copy(q).start()

    def send_group(self, q):
        self.pair_copy(q).wait_recv()
        for g in range(0, GROUP, 2):
            came = self.prcv[q, g * ROWS : (g + 2) * ROWS, :].astype(F32)
            for i in range(2):
                both = self.rows(q, g + i, self.axis.pair) + came[i * ROWS : (i + 1) * ROWS]
                self.gsnd[q, g + i] = fold(both).astype(BF16)
        each_peer(lambda k: self.group_copy(q, k).start())

    def total(self, q):
        each_peer(lambda k: self.group_copy(q, k).wait_recv())
        total = self.gsnd[q, self.axis.group].astype(F32)
        for k in range(1, GROUP):
            total = total + self.grcv[q, k].astype(F32)
        return total

    def drain(self, q):
        self.pair_copy(q).wait_send()
        each_peer(lambda k: self.group_copy(q, k).wait_send())


class Gather:
    def __init__(self, axis, refs):
        self.axis = axis
        self.held, self.pss, self.prs, self.gss, self.grs = refs

    @staticmethod
    def scratch(chunks, width):
        return [
            pltpu.VMEM((chunks, 2, GROUP, 2 * ROWS, width // 2), BF16),
            pltpu.SemaphoreType.DMA((chunks,)),
            pltpu.SemaphoreType.DMA((chunks,)),
            pltpu.SemaphoreType.DMA((chunks, GROUP)),
            pltpu.SemaphoreType.DMA((chunks, GROUP)),
        ]

    def pair_copy(self, q):
        mine = self.held.at[q, self.axis.pair]
        return remote(mine, mine, self.pss.at[q], self.prs.at[q], self.axis.partner())

    def group_copy(self, q, k):
        mine = self.held.at[q, self.axis.pair, self.axis.group]
        return remote(mine, mine, self.gss.at[q, k], self.grs.at[q, k], self.axis.peer(k))

    def send_group(self, q, block):
        self.held[q, self.axis.pair, self.axis.group] = block.astype(BF16)
        each_peer(lambda k: self.group_copy(q, k).start())

    def send_pair(self, q):
        each_peer(lambda k: self.group_copy(q, k).wait_recv())
        self.pair_copy(q).start()

    def wait(self, q):
        self.pair_copy(q).wait_recv()

    def write_rows(self, q, out, width):
        half = width // 2
        for g in range(GROUP):
            even = self.held[q, 0, g].astype(F32)
            odd = self.held[q, 1, g].astype(F32)
            for side in range(2):
                rows = slice(side * ROWS, (side + 1) * ROWS)
                both = jnp.concatenate([even[rows], odd[rows]], axis=0)
                out[g * 16 : g * 16 + 16, side * half : (side + 1) * half] = both.astype(BF16)

    def drain(self, q):
        self.pair_copy(q).wait_send()
        each_peer(lambda k: self.group_copy(q, k).wait_send())


def staged(steps, stages):
    def body(t, carry):
        for start, run in stages:

            @pl.when((t >= start) & (t < start + CHUNKS))
            def _():
                run(t - start)

        return carry

    lax.fori_loop(0, steps, body, 0)


def kernel(n_scatter, n_gather, amps, integrals, vir, occ, one, two, three, *scratch):
    scratch = list(scratch)

    def take(n):
        out = scratch[:n]
        del scratch[:n]
        return out

    block, block_sem, vir_held, vir_sem, den_second, den_first, first, chunk = take(8)
    acc_one, acc_two, acc_three = take(3)
    size = block.shape[0]
    width = size // CHUNKS
    ab, cd = Axis("ab", "cd"), Axis("cd", "ab")
    scatter_one = Scatter(cd, acc_one, take(n_scatter))
    scatter_two = Scatter(ab, acc_two, take(n_scatter))
    scatter_three = Scatter(cd, acc_three, take(n_scatter))
    gather_one = Gather(ab, take(n_gather))
    gather_two = Gather(cd, take(n_gather))
    gather_three = Gather(ab, take(n_gather))

    def load(q):
        rows = pl.ds(pl.multiple_of(q * width, width), width)
        return pltpu.make_async_copy(integrals.at[rows, :], block.at[rows, :], block_sem.at[q])

    def load_vir(i, axis):
        rows = size // LANES
        return pltpu.make_async_copy(
            vir.at[pl.ds(pl.multiple_of(axis.index * rows, rows), rows), :], vir_held.at[i], vir_sem.at[i]
        )

    barrier = pltpu.get_barrier_semaphore()
    for axis in (ab, cd):
        each_peer(
            lambda k: pl.semaphore_signal(barrier, inc=1, device_id=axis.peer(k), device_id_type=MESH)
        )
        pl.semaphore_signal(barrier, inc=1, device_id=axis.partner(), device_id_type=MESH)
    load_vir(0, ab).start()
    load_vir(1, cd).start()
    for q in range(CHUNKS):
        load(q).start()
    mine = fold(amps[...].astype(F32))
    pl.semaphore_wait(barrier, 2 * GROUP)
    gather_one.send_group(0, mine)

    load_vir(0, ab).wait()
    load_vir(1, cd).wait()
    row = lax.broadcasted_iota(jnp.int32, (ROWS, LANES), 0)
    for i, axis, den in ((0, cd, den_second), (1, ab, den_first)):
        levels = jnp.zeros((ROWS, LANES), F32)
        for r in range(ROWS):
            levels = jnp.where(row == r, occ[axis.index * ROWS + r], levels)
        for tile in range(size // LANES):
            per_half = width // 2 // LANES
            q, side, at = tile // (2 * per_half), tile // per_half % 2, tile % per_half
            den[q, side * ROWS : (side + 1) * ROWS, at * LANES : (at + 1) * LANES] = (
                jnp.broadcast_to(vir_held[i, tile : tile + 1, :], (ROWS, LANES)) - levels
            )
    acc_two[...] = jnp.zeros_like(acc_two)
    acc_three[...] = jnp.zeros_like(acc_three)
    gather_one.send_pair(0)
    gather_one.wait(0)
    gather_one.write_rows(0, first, size)

    def columns(q):
        return pl.ds(pl.multiple_of(q * width, width), width)

    def product_one(n):
        load(n).wait()
        acc_one[n] = lax.dot_general(
            first[...], block[columns(n), :], (((1,), (1,)), ((), ())), preferred_element_type=F32
        )
        scatter_one.send_pair(n)

    def finish(scatter, out, den, gather, q):
        total = scatter.total(q)
        out[:, columns(q)] = unfold(total).astype(BF16)
        if gather is not None:
            gather.send_group(q, total / den[q])

    def product(gather, scatter, acc, over_rows, q):
        gather.wait(q)
        gather.write_rows(q, chunk, width)

        def part(n, carry):
            if over_rows:
                acc[n] += jnp.dot(
                    chunk[...], block[columns(q), columns(n)], preferred_element_type=F32
                )
            else:
                acc[n] += lax.dot_general(
                    chunk[...],
                    block[columns(n), columns(q)],
                    (((1,), (1,)), ((), ())),
                    preferred_element_type=F32,
                )

            @pl.when(q == CHUNKS - 1)
            def _():
                scatter.send_pair(n)

            return carry

        lax.fori_loop(0, CHUNKS, part, 0)

    s0, s1, s2, s3, s4 = STAGES
    staged(
        s4 + CHUNKS,
        (
            (s0, product_one),
            (s1, scatter_one.send_group),
            (s2, functools.partial(finish, scatter_one, one, den_second, gather_two)),
            (s3, gather_two.send_pair),
            (s4, functools.partial(product, gather_two, scatter_two, acc_two, True)),
        ),
    )
    staged(
        s4 - s1 + CHUNKS,
        (
            (0, scatter_two.send_group),
            (s2 - s1, functools.partial(finish, scatter_two, two, den_first, gather_three)),
            (s3 - s1, gather_three.send_pair),
            (s4 - s1, functools.partial(product, gather_three, scatter_three, acc_three, False)),
        ),
    )
    staged(
        s2 - s1 + CHUNKS,
        (
            (0, scatter_three.send_group),
            (s2 - s1, functools.partial(finish, scatter_three, three, None, None)),
        ),
    )

    gather_one.drain(0)

    def drain(q, carry):
        for part in (scatter_one, scatter_two, scatter_three, gather_two, gather_three):
            part.drain(q)
        return carry

    lax.fori_loop(0, CHUNKS, drain, 0)


def per_device(amplitudes, integrals, vir_energy, occ_energy):
    size = integrals.shape[0]
    width = size // CHUNKS
    rows = occ_energy.shape[0]
    scatter = Scatter.scratch(CHUNKS, width)
    gather = Gather.scratch(CHUNKS, width)
    vmem = pl.BlockSpec(memory_space=pltpu.VMEM)
    hbm = pl.BlockSpec(memory_space=pl.ANY)
    out = jax.ShapeDtypeStruct(amplitudes.shape, BF16)
    return pl.pallas_call(
        functools.partial(kernel, len(scatter), len(gather)),
        out_shape=(out, out, out),
        in_specs=[vmem, hbm, hbm, pl.BlockSpec(memory_space=pltpu.SMEM)],
        out_specs=(vmem, vmem, vmem),
        scratch_shapes=[
            pltpu.VMEM((size, size), BF16),
            pltpu.SemaphoreType.DMA((CHUNKS,)),
            pltpu.VMEM((2, size // LANES, LANES), F32),
            pltpu.SemaphoreType.DMA((2,)),
            pltpu.VMEM((CHUNKS, 2 * ROWS, width // 2), F32),
            pltpu.VMEM((CHUNKS, 2 * ROWS, width // 2), F32),
            pltpu.VMEM((rows, size), BF16),
            pltpu.VMEM((rows, width), BF16),
        ]
        + [pltpu.VMEM((CHUNKS, rows, width), F32)] * 3
        + scatter * 3
        + Gather.scratch(1, size)
        + gather * 2,
        compiler_params=pltpu.CompilerParams(
            collective_id=0, has_side_effects=True, vmem_limit_bytes=40 * 2**20
        ),
        cost_estimate=pl.CostEstimate(
            flops=6 * rows * size * size, bytes_accessed=2 * size * size, transcendentals=0
        ),
        name="ladder",
    )(amplitudes, integrals, vir_energy.reshape(-1, LANES), occ_energy)


def solution(mesh):
    return jax.shard_map(
        per_device,
        mesh=mesh,
        in_specs=(P("ab", "cd"), P("ab", "cd"), P(), P()),
        out_specs=(P("cd", "ab"), P("ab", "cd"), P("cd", "ab")),
        check_vma=False,
    )
```

```python
import functools

import jax
import jax.numpy as jnp
from jax import lax
from jax.experimental import pallas as pl
from jax.experimental.pallas import tpu as pltpu
from jax.sharding import PartitionSpec as P

MESH = pl.DeviceIdType.MESH
F32 = jnp.float32
BF16 = jnp.bfloat16

GROUP = 8
LANES = 128
ROWS = 8
CHUNKS = 4
TILE = 512
FAR_FIRST = (4, 3, 5, 2, 6, 1, 7)
VMEM_LIMIT = 60 * 2**20
STAGES_ONE = (0, 4, 7, 10, 13)
STAGES_TWO = (0, 3, 6, 9)
STAGES_THREE = (0, 3)
EARLY = 2


class Axis:
    def __init__(self, name, other):
        self.name = name
        self.index = lax.axis_index(name)
        self.other = lax.axis_index(other)
        self.group = lax.div(self.index, 2)
        self.pair = lax.rem(self.index, 2)
        self.groups = [lax.rem(self.group + k, GROUP) for k in range(GROUP)]
        self.peers = [self.device(g * 2 + self.pair) for g in self.groups]

    def device(self, index):
        return (index, self.other) if self.name == "ab" else (self.other, index)

    def peer_group(self, k):
        return self.groups[k]

    def peer(self, k):
        return self.peers[k]

    def partner(self):
        return self.device(self.group * 2 + 1 - self.pair)


def remote(src, dst, send, recv, device):
    return pltpu.make_async_remote_copy(
        src_ref=src, dst_ref=dst, send_sem=send, recv_sem=recv, device_id=device, device_id_type=MESH
    )


def each_peer(body):
    for k in FAR_FIRST:
        body(k)


def wait_bytes(ref, sem):
    pltpu.make_async_copy(ref, ref, sem).wait()


def fold(block):
    half = block.shape[1] // 2
    return jnp.concatenate([block[:, :half], block[:, half:]], axis=0)


def unfold(block):
    return jnp.concatenate([block[:ROWS], block[ROWS:]], axis=1)


class Scatter:
    def __init__(self, axis, acc, refs):
        self.axis, self.acc = axis, acc
        self.psnd, self.prcv, self.gsnd, self.grcv, self.sent, self.came = refs

    @staticmethod
    def scratch(chunks, width):
        return [
            pltpu.VMEM((chunks, GROUP * ROWS, width), BF16),
            pltpu.VMEM((chunks, GROUP * ROWS, width), BF16),
            pltpu.VMEM((chunks, GROUP, 2 * ROWS, width // 2), BF16),
            pltpu.VMEM((chunks, GROUP - 1, 2 * ROWS, width // 2), BF16),
            pltpu.SemaphoreType.DMA((2,)),
            pltpu.SemaphoreType.DMA((2, chunks)),
        ]

    def rows(self, q, g, pair):
        width = self.psnd.shape[-1]
        return self.acc[
            pl.ds(pl.multiple_of(g * 16 + pair * ROWS, ROWS), ROWS),
            pl.ds(pl.multiple_of(q * width, width), width),
        ]

    def pair_copy(self, q):
        return remote(
            self.psnd.at[q], self.prcv.at[q], self.sent.at[0], self.came.at[0, q], self.axis.partner()
        )

    def group_copy(self, q, k):
        return remote(
            self.gsnd.at[q, self.axis.peer_group(k)],
            self.grcv.at[q, k - 1],
            self.sent.at[1],
            self.came.at[1, q],
            self.axis.peer(k),
        )

    def send_pair(self, q):
        other = 1 - self.axis.pair
        for g in range(0, GROUP, 2):
            two = jnp.concatenate([self.rows(q, g, other), self.rows(q, g + 1, other)], axis=0)
            self.psnd[q, g * ROWS : (g + 2) * ROWS, :] = two.astype(BF16)
        self.pair_copy(q).start()

    def send_group(self, q):
        wait_bytes(self.prcv.at[q], self.came.at[0, q])
        for g in range(0, GROUP, 2):
            came = self.prcv[q, g * ROWS : (g + 2) * ROWS, :].astype(F32)
            for i in range(2):
                both = self.rows(q, g + i, self.axis.pair) + came[i * ROWS : (i + 1) * ROWS]
                self.gsnd[q, g + i] = fold(both).astype(BF16)
        each_peer(lambda k: self.group_copy(q, k).start())

    def total(self, q):
        wait_bytes(self.grcv.at[q], self.came.at[1, q])
        total = self.gsnd[q, self.axis.group].astype(F32)
        for k in range(GROUP - 1):
            total = total + self.grcv[q, k].astype(F32)
        return total

    def drain(self, pairs=True, groups=True):
        if pairs:
            wait_bytes(self.psnd, self.sent.at[0])
        if groups:
            wait_bytes(self.grcv, self.sent.at[1])


class Gather:
    def __init__(self, axis, refs):
        self.axis = axis
        self.held, self.sent, self.came = refs

    @staticmethod
    def scratch(chunks, width):
        return [
            pltpu.VMEM((chunks, 2, GROUP, 2 * ROWS, width // 2), BF16),
            pltpu.SemaphoreType.DMA((2,)),
            pltpu.SemaphoreType.DMA((2, chunks)),
        ]

    def pair_copy(self, q):
        mine = self.held.at[q, self.axis.pair]
        return remote(mine, mine, self.sent.at[0], self.came.at[0, q], self.axis.partner())

    def group_copy(self, q, k):
        mine = self.held.at[q, self.axis.pair, self.axis.group]
        return remote(mine, mine, self.sent.at[1], self.came.at[1, q], self.axis.peer(k))

    def send_group(self, q, block):
        self.held[q, self.axis.pair, self.axis.group] = block.astype(BF16)
        each_peer(lambda k: self.group_copy(q, k).start())

    def send_pair(self, q):
        wait_bytes(self.held.at[q, 0, pl.ds(0, GROUP - 1)], self.came.at[1, q])
        self.pair_copy(q).start()

    def wait(self, q):
        wait_bytes(self.held.at[q, 0], self.came.at[0, q])

    def write_rows(self, q, out, start):
        half = self.held.shape[-1]
        for g in range(GROUP):
            even = self.held[q, 0, g].astype(F32)
            odd = self.held[q, 1, g].astype(F32)
            for side in range(2):
                rows = slice(side * ROWS, (side + 1) * ROWS)
                both = jnp.concatenate([even[rows], odd[rows]], axis=0)
                at = start + side * half
                out[g * 16 : g * 16 + 16, at : at + half] = both.astype(BF16)

    def drain(self):
        wait_bytes(self.held.at[:, 0], self.sent.at[0])
        wait_bytes(self.held.at[:, 0, pl.ds(0, GROUP - 1)], self.sent.at[1])


def staged(steps, stages):
    def body(t, carry):
        for start, run in stages:

            @pl.when((t >= start) & (t < start + CHUNKS))
            def _():
                run(t - start)

        return carry

    lax.fori_loop(0, steps, body, 0)


def kernel(n_scatter, n_gather, amps, integrals, vir, occ, one, two, three, *scratch):
    outs = one, two, three
    scratch = list(scratch)

    def take(n):
        out = scratch[:n]
        del scratch[:n]
        return out

    amps_held, occ_held, block, block_sem, vir_held, vir_sem, den_second, den_first, first, chunk, out_held, out_sem = take(12)
    acc_one, acc_two, acc_three = take(3)
    size = block.shape[0]
    width = size // CHUNKS
    tiles, per_tile = size // TILE, TILE // width
    ab, cd = Axis("ab", "cd"), Axis("cd", "ab")
    scatter_one = Scatter(cd, acc_one, take(n_scatter))
    scatter_two = Scatter(ab, acc_two, take(n_scatter))
    scatter_three = Scatter(cd, acc_three, take(n_scatter))
    gather_one = Gather(ab, take(n_gather))
    gather_two = Gather(cd, take(n_gather))
    gather_three = Gather(ab, take(n_gather))

    def load(q):
        rows = pl.ds(pl.multiple_of(q * TILE, TILE), TILE)
        return pltpu.make_async_copy(integrals.at[rows, :], block.at[rows, :], block_sem.at[q])

    def load_vir(i, axis):
        rows = size // LANES
        return pltpu.make_async_copy(
            vir.at[pl.ds(pl.multiple_of(axis.index * rows, rows), rows), :], vir_held.at[i], vir_sem.at[i]
        )

    load_amps = pltpu.make_async_copy(amps, amps_held, vir_sem.at[2])
    load_occ = pltpu.make_async_copy(occ, occ_held, vir_sem.at[3])

    barrier = pltpu.get_barrier_semaphore()
    for axis in (ab, cd):
        each_peer(
            lambda k: pl.semaphore_signal(barrier, inc=1, device_id=axis.peer(k), device_id_type=MESH)
        )
        pl.semaphore_signal(barrier, inc=1, device_id=axis.partner(), device_id_type=MESH)
    load_amps.start()
    load_vir(0, ab).start()
    load_vir(1, cd).start()
    load_occ.start()
    for q in range(EARLY):
        load(q).start()
    load_amps.wait()
    mine = fold(amps_held[...].astype(F32))
    pl.semaphore_wait(barrier, 2 * GROUP)
    gather_one.send_group(0, mine)
    for q in range(EARLY, tiles):
        load(q).start()

    load_vir(0, ab).wait()
    load_vir(1, cd).wait()
    load_occ.wait()
    row = lax.broadcasted_iota(jnp.int32, (ROWS, LANES), 0)
    for i, axis, den in ((0, cd, den_second), (1, ab, den_first)):
        levels = jnp.zeros((ROWS, LANES), F32)
        for r in range(ROWS):
            levels = jnp.where(row == r, occ_held[axis.index * ROWS + r], levels)
        for lane_tile in range(size // LANES):
            per_half = width // 2 // LANES
            part = lane_tile // per_half
            q, side, at = part // 2, part % 2, lane_tile % per_half
            den[q, side * ROWS : (side + 1) * ROWS, at * LANES : (at + 1) * LANES] = (
                jnp.broadcast_to(vir_held[i, lane_tile : lane_tile + 1, :], (ROWS, LANES)) - levels
            )
    acc_two[...] = jnp.zeros_like(acc_two)
    acc_three[...] = jnp.zeros_like(acc_three)
    gather_one.send_pair(0)
    gather_one.wait(0)
    gather_one.write_rows(0, first, 0)

    def columns(q):
        return pl.ds(pl.multiple_of(q * width, width), width)

    def tile(n):
        return pl.ds(pl.multiple_of(n * TILE, TILE), TILE)

    def product_one(q):
        @pl.when(lax.rem(q, per_tile) == 0)
        def _():
            n = lax.div(q, per_tile)
            load(n).wait()
            acc_one[:, tile(n)] = lax.dot_general(
                first[...], block[tile(n), :], (((1,), (1,)), ((), ())), preferred_element_type=F32
            )
            for i in range(per_tile):
                scatter_one.send_pair(q + i)

    def store(i):
        return pltpu.make_async_copy(out_held.at[i], outs[i], out_sem.at[i])

    def finish(scatter, i, den, gather, q):
        total = scatter.total(q)
        if gather is not None:
            gather.send_group(q, total / den[q])
        out_held[i, :, columns(q)] = unfold(total).astype(BF16)

        @pl.when(q == CHUNKS - 1)
        def _():
            store(i).start()

    def product(gather, scatter, acc, over_rows, q):
        gather.wait(q)
        for i in range(per_tile):

            @pl.when(lax.rem(q, per_tile) == i)
            def _():
                gather.write_rows(q, chunk, i * width)

        @pl.when(lax.rem(q, per_tile) == per_tile - 1)
        def _():
            m = lax.div(q, per_tile)

            def part(n, carry):
                if over_rows:
                    acc[:, tile(n)] += jnp.dot(
                        chunk[...], block[tile(m), tile(n)], preferred_element_type=F32
                    )
                else:
                    acc[:, tile(n)] += lax.dot_general(
                        chunk[...],
                        block[tile(n), tile(m)],
                        (((1,), (1,)), ((), ())),
                        preferred_element_type=F32,
                    )

                @pl.when(q == CHUNKS - 1)
                def _():
                    for i in range(per_tile):
                        scatter.send_pair(n * per_tile + i)

                return carry

            lax.fori_loop(0, tiles, part, 0)

    s0, s1, s2, s3, s4 = STAGES_ONE
    staged(
        s4 + CHUNKS,
        (
            (s0, product_one),
            (s1, scatter_one.send_group),
            (s2, functools.partial(finish, scatter_one, 0, den_second, gather_two)),
            (s3, gather_two.send_pair),
            (s4, functools.partial(product, gather_two, scatter_two, acc_two, True)),
        ),
    )
    s0, s1, s2, s3 = STAGES_TWO
    staged(
        s3 + CHUNKS,
        (
            (s0, scatter_two.send_group),
            (s1, functools.partial(finish, scatter_two, 1, den_first, gather_three)),
            (s2, gather_three.send_pair),
            (s3, functools.partial(product, gather_three, scatter_three, acc_three, False)),
        ),
    )
    s0, s1 = STAGES_THREE
    staged(
        s1 + CHUNKS,
        (
            (s0, scatter_three.send_group),
            (s1, functools.partial(finish, scatter_three, 2, None, None)),
        ),
    )

    for part in (gather_one, gather_two, gather_three, scatter_one, scatter_two, scatter_three):
        part.drain()
    for i in range(3):
        store(i).wait()


def hand_on(*refs):
    sources, targets, held, sems = refs[:3], refs[3:6], refs[6], refs[7]
    came = [pltpu.make_async_copy(sources[i], held.at[i], sems.at[i]) for i in range(3)]
    gone = [pltpu.make_async_copy(held.at[i], targets[i], sems.at[i]) for i in range(3)]
    for copy in came:
        copy.start()
    for i in range(3):
        came[i].wait()
        gone[i].start()
    for copy in gone:
        copy.wait()


def per_device(amplitudes, integrals, vir_energy, occ_energy):
    size = integrals.shape[0]
    width = size // CHUNKS
    rows = occ_energy.shape[0]
    scatter = Scatter.scratch(CHUNKS, width)
    gather = Gather.scratch(CHUNKS, width)
    hbm = pl.BlockSpec(memory_space=pltpu.HBM)
    out = jax.ShapeDtypeStruct(amplitudes.shape, BF16)
    ladders = pl.pallas_call(
        functools.partial(kernel, len(scatter), len(gather)),
        out_shape=(out, out, out),
        in_specs=[hbm] * 4,
        out_specs=(hbm, hbm, hbm),
        scratch_shapes=[
            pltpu.VMEM(amplitudes.shape, BF16),
            pltpu.SMEM((rows,), F32),
            pltpu.VMEM((size, size), BF16),
            pltpu.SemaphoreType.DMA((size // TILE,)),
            pltpu.VMEM((2, size // LANES, LANES), F32),
            pltpu.SemaphoreType.DMA((4,)),
            pltpu.VMEM((CHUNKS, 2 * ROWS, width // 2), F32),
            pltpu.VMEM((CHUNKS, 2 * ROWS, width // 2), F32),
            pltpu.VMEM((rows, size), BF16),
            pltpu.VMEM((rows, TILE), BF16),
            pltpu.VMEM((3,) + amplitudes.shape, BF16),
            pltpu.SemaphoreType.DMA((3,)),
        ]
        + [pltpu.VMEM((rows, size), F32)] * 3
        + scatter * 3
        + Gather.scratch(1, size)
        + gather * 2,
        compiler_params=pltpu.CompilerParams(
            collective_id=0, has_side_effects=True, vmem_limit_bytes=VMEM_LIMIT
        ),
        cost_estimate=pl.CostEstimate(
            flops=6 * rows * size * size, bytes_accessed=2 * size * size, transcendentals=0
        ),
        name="ladder",
    )(amplitudes, integrals, vir_energy.reshape(-1, LANES), occ_energy)
    return pl.pallas_call(
        hand_on,
        out_shape=(out, out, out),
        in_specs=[hbm] * 3,
        out_specs=(hbm,) * 3,
        scratch_shapes=[pltpu.VMEM((3,) + amplitudes.shape, BF16), pltpu.SemaphoreType.DMA((3,))],
        name="hand_on",
    )(*ladders)


def solution(mesh):
    return jax.shard_map(
        per_device,
        mesh=mesh,
        in_specs=(P("ab", "cd"), P("ab", "cd"), P(), P()),
        out_specs=(P("cd", "ab"), P("ab", "cd"), P("cd", "ab")),
        check_vma=False,
    )
```

```python
import functools

import jax
import jax.numpy as jnp
from jax import lax
from jax.experimental import pallas as pl
from jax.experimental.pallas import tpu as pltpu
from jax.sharding import PartitionSpec as P

MESH = pl.DeviceIdType.MESH
F32 = jnp.float32
BF16 = jnp.bfloat16

GROUP = 8
LANES = 128
ROWS = 8
CHUNKS = 4
TILE = 512
FAR_FIRST = (4, 3, 5, 2, 6, 1, 7)
VMEM_LIMIT = 60 * 2**20
STAGES_ONE = (0, 4, 7, 10, 13)
STAGES_TWO = (0, 3, 6, 9)
STAGES_THREE = (0, 4)
AMP_CHUNKS = 1
WIDE_ONE = (2,)
WIDE_THREE = (3,)


class Axis:
    def __init__(self, name, other):
        self.name = name
        self.index = lax.axis_index(name)
        self.other = lax.axis_index(other)
        self.group = lax.div(self.index, 2)
        self.pair = lax.rem(self.index, 2)
        self.groups = [lax.rem(self.group + k, GROUP) for k in range(GROUP)]
        self.peers = [self.device(g * 2 + self.pair) for g in self.groups]

    def device(self, index):
        return (index, self.other) if self.name == "ab" else (self.other, index)

    def partner(self):
        return self.device(self.group * 2 + 1 - self.pair)


def remote(src, dst, send, recv, device):
    return pltpu.make_async_remote_copy(
        src_ref=src, dst_ref=dst, send_sem=send, recv_sem=recv, device_id=device, device_id_type=MESH
    )


def each_peer(body):
    for k in FAR_FIRST:
        body(k)


def dot(left, right):
    return jnp.dot(left, right, preferred_element_type=F32)


def wait_bytes(ref, sem):
    pltpu.make_async_copy(ref, ref, sem).wait()


def fold(block):
    half = block.shape[1] // 2
    return jnp.concatenate([block[:, :half], block[:, half:]], axis=0)


def unfold(block):
    return jnp.concatenate([block[:ROWS], block[ROWS:]], axis=1)


class Scatter:
    def __init__(self, axis, acc, wide, refs):
        self.axis, self.acc, self.wide = axis, acc, wide
        self.psnd, self.prcv, self.gsnd, self.grcv, self.sent, self.came = refs[:6]
        if wide:
            self.wsnd, self.wrcv, self.wpsnd, self.wprcv, self.wsum, self.wsent, self.wcame = refs[6:]
        self.width = self.psnd.shape[-1]

    @staticmethod
    def scratch(chunks, width, wide):
        out = [
            pltpu.VMEM((chunks, GROUP * ROWS, width), BF16),
            pltpu.VMEM((chunks, GROUP * ROWS, width), BF16),
            pltpu.VMEM((chunks, GROUP, 2 * ROWS, width // 2), BF16),
            pltpu.VMEM((chunks, GROUP - 1, 2 * ROWS, width // 2), BF16),
            pltpu.SemaphoreType.DMA((2,)),
            pltpu.SemaphoreType.DMA((2, chunks)),
        ]
        if wide:
            n = len(wide)
            out += [
                pltpu.VMEM((n, GROUP, 2 * ROWS, width), BF16),
                pltpu.VMEM((n, GROUP - 1, 2 * ROWS, width), BF16),
                pltpu.VMEM((n, 2 * ROWS, width // 2), BF16),
                pltpu.VMEM((n, 2 * ROWS, width // 2), BF16),
                pltpu.VMEM((n, 2 * ROWS, width // 2), F32),
                pltpu.SemaphoreType.DMA((2,)),
                pltpu.SemaphoreType.DMA((2, n)),
            ]
        return out

    def columns(self, q):
        return pl.ds(pl.multiple_of(q * self.width, self.width), self.width)

    def rows(self, q, g, pair):
        at = pl.ds(pl.multiple_of(g * 16 + pair * ROWS, ROWS), ROWS)
        return self.acc[at, self.columns(q)]

    def either(self, q, narrow, wide):
        is_wide = False
        for i, w in enumerate(self.wide):
            pl.when(q == w)(functools.partial(wide, i))
            is_wide = (q == w) | is_wide
        if self.wide:
            pl.when(jnp.logical_not(is_wide))(narrow)
        else:
            narrow()

    def pair_copy(self, q):
        return remote(
            self.psnd.at[q], self.prcv.at[q], self.sent.at[0], self.came.at[0, q], self.axis.partner()
        )

    def group_copy(self, q, k):
        return remote(
            self.gsnd.at[q, self.axis.groups[k]],
            self.grcv.at[q, k - 1],
            self.sent.at[1],
            self.came.at[1, q],
            self.axis.peers[k],
        )

    def wide_group_copy(self, i, k):
        return remote(
            self.wsnd.at[i, self.axis.groups[k]],
            self.wrcv.at[i, k - 1],
            self.wsent.at[0],
            self.wcame.at[0, i],
            self.axis.peers[k],
        )

    def wide_pair_copy(self, i):
        return remote(
            self.wpsnd.at[i], self.wprcv.at[i], self.wsent.at[1], self.wcame.at[1, i], self.axis.partner()
        )

    def begin(self, q):
        def narrow():
            other = 1 - self.axis.pair
            for g in range(0, GROUP, 2):
                two = jnp.concatenate([self.rows(q, g, other), self.rows(q, g + 1, other)], axis=0)
                self.psnd[q, g * ROWS : (g + 2) * ROWS, :] = two.astype(BF16)
            self.pair_copy(q).start()

        def wide(i):
            def send(k):
                g = self.axis.groups[k]
                both = pl.ds(pl.multiple_of(g * 16, 16), 16)
                self.wsnd[i, g] = self.acc[both, self.columns(q)].astype(BF16)
                if k:
                    self.wide_group_copy(i, k).start()

            each_peer(send)
            send(0)

        self.either(q, narrow, wide)

    def middle(self, q):
        def narrow():
            wait_bytes(self.prcv.at[q], self.came.at[0, q])
            for g in range(0, GROUP, 2):
                came = self.prcv[q, g * ROWS : (g + 2) * ROWS, :].astype(F32)
                for i in range(2):
                    both = self.rows(q, g + i, self.axis.pair) + came[i * ROWS : (i + 1) * ROWS]
                    self.gsnd[q, g + i] = fold(both).astype(BF16)
            each_peer(lambda k: self.group_copy(q, k).start())

        def wide(i):
            wait_bytes(self.wrcv.at[i], self.wcame.at[0, i])
            total = self.wsnd[i, self.axis.group].astype(F32)
            for k in range(GROUP - 1):
                total = total + self.wrcv[i, k].astype(F32)
            even, odd = fold(total[:ROWS]), fold(total[ROWS:])
            is_even = self.axis.pair == 0
            self.wpsnd[i] = jnp.where(is_even, odd, even).astype(BF16)
            self.wsum[i] = jnp.where(is_even, even, odd)
            self.wide_pair_copy(i).start()

        self.either(q, narrow, wide)

    def end(self, q, use):
        def narrow():
            wait_bytes(self.grcv.at[q], self.came.at[1, q])
            total = self.gsnd[q, self.axis.group].astype(F32)
            for k in range(GROUP - 1):
                total = total + self.grcv[q, k].astype(F32)
            use(total)

        def wide(i):
            wait_bytes(self.wprcv.at[i], self.wcame.at[1, i])
            use(self.wsum[i] + self.wprcv[i].astype(F32))

        self.either(q, narrow, wide)

    def drain(self):
        count = self.psnd.shape[0] - len(self.wide)
        wait_bytes(self.psnd.at[pl.ds(0, count)], self.sent.at[0])
        wait_bytes(self.grcv.at[pl.ds(0, count)], self.sent.at[1])
        if self.wide:
            wait_bytes(self.wrcv, self.wsent.at[0])
            wait_bytes(self.wpsnd, self.wsent.at[1])


class Gather:
    def __init__(self, axis, refs):
        self.axis = axis
        self.held, self.sent, self.came = refs

    @staticmethod
    def scratch(chunks, width):
        return [
            pltpu.VMEM((chunks, 2, GROUP, 2 * ROWS, width // 2), BF16),
            pltpu.SemaphoreType.DMA((2,)),
            pltpu.SemaphoreType.DMA((2, chunks)),
        ]

    def pair_copy(self, q):
        mine = self.held.at[q, self.axis.pair]
        return remote(mine, mine, self.sent.at[0], self.came.at[0, q], self.axis.partner())

    def group_copy(self, q, k):
        mine = self.held.at[q, self.axis.pair, self.axis.group]
        return remote(mine, mine, self.sent.at[1], self.came.at[1, q], self.axis.peers[k])

    def send_group(self, q, block):
        self.held[q, self.axis.pair, self.axis.group] = block.astype(BF16)
        each_peer(lambda k: self.group_copy(q, k).start())

    def send_pair(self, q):
        wait_bytes(self.held.at[q, 0, pl.ds(0, GROUP - 1)], self.came.at[1, q])
        self.pair_copy(q).start()

    def wait(self, q):
        wait_bytes(self.held.at[q, 0], self.came.at[0, q])

    def write_rows(self, q, out, start):
        half = self.held.shape[-1]
        for g in range(GROUP):
            even = self.held[q, 0, g].astype(F32)
            odd = self.held[q, 1, g].astype(F32)
            for side in range(2):
                rows = slice(side * ROWS, (side + 1) * ROWS)
                both = jnp.concatenate([even[rows], odd[rows]], axis=0)
                at = start + side * half
                out[g * 16 : g * 16 + 16, at : at + half] = both.astype(BF16)

    def drain(self):
        wait_bytes(self.held.at[:, 0], self.sent.at[0])
        wait_bytes(self.held.at[:, 0, pl.ds(0, GROUP - 1)], self.sent.at[1])


def staged(steps, stages):
    def body(t, carry):
        for start, run in stages:

            @pl.when((t >= start) & (t < start + CHUNKS))
            def _():
                run(t - start)

        return carry

    lax.fori_loop(0, steps, body, 0)


def kernel(amps, integrals, vir, occ, one, two, three, *scratch):
    outs = one, two, three
    scratch = list(scratch)

    def take(n):
        out = scratch[:n]
        del scratch[:n]
        return out

    amps_held, occ_held, block, turned, block_sem, vir_held, vir_sem, den_second, den_first, first, chunk, out_held, out_sem = take(13)
    acc_one, acc_two, acc_three = take(3)
    rows, size = first.shape
    width = size // CHUNKS
    tiles, per_tile = size // TILE, TILE // width
    ab, cd = Axis("ab", "cd"), Axis("cd", "ab")
    scatter_one = Scatter(cd, acc_one, WIDE_ONE, take(13 if WIDE_ONE else 6))
    scatter_two = Scatter(ab, acc_two, (), take(6))
    scatter_three = Scatter(cd, acc_three, WIDE_THREE, take(13 if WIDE_THREE else 6))
    gather_one = Gather(ab, take(3))
    gather_two = Gather(cd, take(3))
    gather_three = Gather(ab, take(3))

    def load(q):
        rows = pl.ds(pl.multiple_of(q * TILE, TILE), TILE)
        return pltpu.make_async_copy(integrals.at[rows, :], block.at[rows, :], block_sem.at[q])

    def load_vir(i, axis):
        rows = size // LANES
        return pltpu.make_async_copy(
            vir.at[pl.ds(pl.multiple_of(axis.index * rows, rows), rows), :], vir_held.at[i], vir_sem.at[i]
        )

    load_amps = pltpu.make_async_copy(amps, amps_held, vir_sem.at[2])
    load_occ = pltpu.make_async_copy(occ, occ_held, vir_sem.at[3])

    barrier = pltpu.get_barrier_semaphore()
    for axis in (ab, cd):
        each_peer(
            lambda k: pl.semaphore_signal(barrier, inc=1, device_id=axis.peers[k], device_id_type=MESH)
        )
        pl.semaphore_signal(barrier, inc=1, device_id=axis.partner(), device_id_type=MESH)
    load_amps.start()
    load_vir(0, ab).start()
    load_vir(1, cd).start()
    load_occ.start()
    for q in range(tiles):
        load(q).start()
    load_amps.wait()
    amp_width = size // AMP_CHUNKS
    pl.semaphore_wait(barrier, 2 * GROUP)
    for i in range(AMP_CHUNKS):
        part = amps_held[:, i * amp_width : (i + 1) * amp_width]
        gather_one.send_group(i, fold(part.astype(F32)))

    load_vir(0, ab).wait()
    load_vir(1, cd).wait()
    load_occ.wait()
    row = lax.broadcasted_iota(jnp.int32, (ROWS, LANES), 0)
    for i, axis, den in ((0, cd, den_second), (1, ab, den_first)):
        levels = jnp.zeros((ROWS, LANES), F32)
        for r in range(ROWS):
            levels = jnp.where(row == r, occ_held[axis.index * ROWS + r], levels)
        for lane_tile in range(size // LANES):
            per_half = width // 2 // LANES
            part = lane_tile // per_half
            q, side, at = part // 2, part % 2, lane_tile % per_half
            den[q, side * ROWS : (side + 1) * ROWS, at * LANES : (at + 1) * LANES] = (
                jnp.broadcast_to(vir_held[i, lane_tile : lane_tile + 1, :], (ROWS, LANES)) - levels
            )
    acc_two[...] = jnp.zeros_like(acc_two)
    acc_three[...] = jnp.zeros_like(acc_three)
    def turn(r):
        load(r).wait()

        def part(c, carry):
            to, at = (pl.ds(pl.multiple_of(i * TILE, TILE), TILE) for i in (r, c))
            turned[at, to] = block[to, at].T
            return carry

        lax.fori_loop(0, tiles, part, 0)

    for r in range(tiles):
        turn(r)
    for i in range(AMP_CHUNKS):
        gather_one.send_pair(i)
    first_tile = jnp.zeros((rows, TILE), F32)
    for i in range(AMP_CHUNKS):
        gather_one.wait(i)
        gather_one.write_rows(i, first, i * amp_width)
        at = slice(i * amp_width, (i + 1) * amp_width)
        first_tile += dot(first[:, at], turned[at, :TILE])
    acc_one[:, :TILE] = first_tile

    def columns(q):
        return pl.ds(pl.multiple_of(q * width, width), width)

    def tile(n):
        return pl.ds(pl.multiple_of(n * TILE, TILE), TILE)

    def product_one(q):
        @pl.when(lax.rem(q, per_tile) == 0)
        def _():
            n = lax.div(q, per_tile)

            @pl.when(n > 0)
            def _():
                acc_one[:, tile(n)] = dot(first[...], turned[:, tile(n)])

            for i in range(per_tile):
                scatter_one.begin(q + i)

    def store(i):
        return pltpu.make_async_copy(out_held.at[i], outs[i], out_sem.at[i])

    def finish(scatter, i, den, gather, q):
        def use(total):
            if gather is not None:
                gather.send_group(q, total / den[q])
            out_held[i, :, columns(q)] = unfold(total).astype(BF16)

        scatter.end(q, use)

        @pl.when(q == CHUNKS - 1)
        def _():
            store(i).start()

    def product(gather, scatter, acc, integrals, q):
        gather.wait(q)
        for i in range(per_tile):

            @pl.when(lax.rem(q, per_tile) == i)
            def _():
                gather.write_rows(q, chunk, i * width)

        @pl.when(lax.rem(q, per_tile) == per_tile - 1)
        def _():
            m = lax.div(q, per_tile)

            def part(n, carry):
                acc[:, tile(n)] += dot(chunk[...], integrals[tile(m), tile(n)])

                @pl.when(q == CHUNKS - 1)
                def _():
                    for i in range(per_tile):
                        scatter.begin(n * per_tile + i)

                return carry

            lax.fori_loop(0, tiles, part, 0)

    s0, s1, s2, s3, s4 = STAGES_ONE
    staged(
        s4 + CHUNKS,
        (
            (s0, product_one),
            (s1, scatter_one.middle),
            (s2, functools.partial(finish, scatter_one, 0, den_second, gather_two)),
            (s3, gather_two.send_pair),
            (s4, functools.partial(product, gather_two, scatter_two, acc_two, block)),
        ),
    )
    s0, s1, s2, s3 = STAGES_TWO
    staged(
        s3 + CHUNKS,
        (
            (s0, scatter_two.middle),
            (s1, functools.partial(finish, scatter_two, 1, den_first, gather_three)),
            (s2, gather_three.send_pair),
            (s3, functools.partial(product, gather_three, scatter_three, acc_three, turned)),
        ),
    )
    s0, s1 = STAGES_THREE
    staged(
        s1 + CHUNKS,
        (
            (s0, scatter_three.middle),
            (s1, functools.partial(finish, scatter_three, 2, None, None)),
        ),
    )

    for part in (gather_one, gather_two, gather_three, scatter_one, scatter_two, scatter_three):
        part.drain()
    for i in range(3):
        store(i).wait()


def hand_on(*refs):
    sources, targets, held, sems = refs[:3], refs[3:6], refs[6], refs[7]
    came = [pltpu.make_async_copy(sources[i], held.at[i], sems.at[i]) for i in range(3)]
    gone = [pltpu.make_async_copy(held.at[i], targets[i], sems.at[i]) for i in range(3)]
    for copy in came:
        copy.start()
    for i in range(3):
        came[i].wait()
        gone[i].start()
    for copy in gone:
        copy.wait()


def per_device(amplitudes, integrals, vir_energy, occ_energy):
    size = integrals.shape[0]
    width = size // CHUNKS
    rows = occ_energy.shape[0]
    hbm = pl.BlockSpec(memory_space=pltpu.HBM)
    out = jax.ShapeDtypeStruct(amplitudes.shape, BF16)
    ladders = pl.pallas_call(
        kernel,
        out_shape=(out, out, out),
        in_specs=[hbm] * 4,
        out_specs=(hbm, hbm, hbm),
        scratch_shapes=[
            pltpu.VMEM(amplitudes.shape, BF16),
            pltpu.SMEM((rows,), F32),
            pltpu.VMEM((size, size), BF16),
            pltpu.VMEM((size, size), BF16),
            pltpu.SemaphoreType.DMA((size // TILE,)),
            pltpu.VMEM((2, size // LANES, LANES), F32),
            pltpu.SemaphoreType.DMA((4,)),
            pltpu.VMEM((CHUNKS, 2 * ROWS, width // 2), F32),
            pltpu.VMEM((CHUNKS, 2 * ROWS, width // 2), F32),
            pltpu.VMEM((rows, size), BF16),
            pltpu.VMEM((rows, TILE), BF16),
            pltpu.VMEM((3,) + amplitudes.shape, BF16),
            pltpu.SemaphoreType.DMA((3,)),
        ]
        + [pltpu.VMEM((rows, size), F32)] * 3
        + Scatter.scratch(CHUNKS, width, WIDE_ONE)
        + Scatter.scratch(CHUNKS, width, ())
        + Scatter.scratch(CHUNKS, width, WIDE_THREE)
        + Gather.scratch(AMP_CHUNKS, size // AMP_CHUNKS)
        + Gather.scratch(CHUNKS, width) * 2,
        compiler_params=pltpu.CompilerParams(
            collective_id=0, has_side_effects=True, vmem_limit_bytes=VMEM_LIMIT
        ),
        cost_estimate=pl.CostEstimate(
            flops=6 * rows * size * size, bytes_accessed=2 * size * size, transcendentals=0
        ),
        name="ladder",
    )(amplitudes, integrals, vir_energy.reshape(-1, LANES), occ_energy)
    return pl.pallas_call(
        hand_on,
        out_shape=(out, out, out),
        in_specs=[hbm] * 3,
        out_specs=(hbm,) * 3,
        scratch_shapes=[pltpu.VMEM((3,) + amplitudes.shape, BF16), pltpu.SemaphoreType.DMA((3,))],
        name="hand_on",
    )(*ladders)


def solution(mesh):
    return jax.shard_map(
        per_device,
        mesh=mesh,
        in_specs=(P("ab", "cd"), P("ab", "cd"), P(), P()),
        out_specs=(P("cd", "ab"), P("ab", "cd"), P("cd", "ab")),
        check_vma=False,
    )
```

```python
import functools

import jax
import jax.numpy as jnp
import numpy as np
from jax import lax
from jax.experimental import pallas as pl
from jax.experimental.pallas import tpu as pltpu
from jax.sharding import PartitionSpec as P

MESH = pl.DeviceIdType.MESH
F32 = jnp.float32
BF16 = jnp.bfloat16

GROUP = 8
LANES = 128
ROWS = 8
CHUNKS = 4
TILE = 512
FAR_FIRST = (4, 3, 5, 2, 6, 1, 7)
VMEM_LIMIT = 60 * 2**20
STAGES_ONE = (0, 4, 7, 10, 13)
STAGES_TWO = (0, 3, 6, 9)
STAGES_THREE = (0, 4)
AMP_CHUNKS = 1
WIDE_ONE = (2,)
WIDE_THREE = (3,)


class Axis:
    def __init__(self, name, other):
        self.name = name
        self.index = lax.axis_index(name)
        self.other = lax.axis_index(other)
        self.group = lax.div(self.index, 2)
        self.pair = lax.rem(self.index, 2)
        self.groups = [lax.rem(self.group + k, GROUP) for k in range(GROUP)]
        self.peers = [self.device(g * 2 + self.pair) for g in self.groups]

    def device(self, index):
        return (index, self.other) if self.name == "ab" else (self.other, index)

    def partner(self):
        return self.device(self.group * 2 + 1 - self.pair)


def remote(src, dst, send, recv, device):
    return pltpu.make_async_remote_copy(
        src_ref=src, dst_ref=dst, send_sem=send, recv_sem=recv, device_id=device, device_id_type=MESH
    )


def each_peer(body):
    for k in FAR_FIRST:
        body(k)


def dot(left, right):
    return jnp.dot(left, right, preferred_element_type=F32)


def wait_bytes(ref, sem):
    pltpu.make_async_copy(ref, ref, sem).wait()


def fold(block):
    half = block.shape[1] // 2
    return jnp.concatenate([block[:, :half], block[:, half:]], axis=0)


def unfold(block):
    return jnp.concatenate([block[:ROWS], block[ROWS:]], axis=1)


class Scatter:
    def __init__(self, axis, acc, wide, refs):
        self.axis, self.acc, self.wide = axis, acc, wide
        self.psnd, self.prcv, self.gsnd, self.grcv, self.sent, self.came = refs[:6]
        if wide:
            self.wsnd, self.wrcv, self.wpsnd, self.wprcv, self.wsum, self.wsent, self.wcame = refs[6:]
        self.width = self.psnd.shape[-1]

    @staticmethod
    def scratch(chunks, width, wide):
        out = [
            pltpu.VMEM((chunks, GROUP * ROWS, width), BF16),
            pltpu.VMEM((chunks, GROUP * ROWS, width), BF16),
            pltpu.VMEM((chunks, GROUP, 2 * ROWS, width // 2), BF16),
            pltpu.VMEM((chunks, GROUP - 1, 2 * ROWS, width // 2), BF16),
            pltpu.SemaphoreType.DMA((2,)),
            pltpu.SemaphoreType.DMA((2, chunks)),
        ]
        if wide:
            n = len(wide)
            out += [
                pltpu.VMEM((n, GROUP, 2 * ROWS, width), BF16),
                pltpu.VMEM((n, GROUP - 1, 2 * ROWS, width), BF16),
                pltpu.VMEM((n, 2 * ROWS, width // 2), BF16),
                pltpu.VMEM((n, 2 * ROWS, width // 2), BF16),
                pltpu.VMEM((n, 2 * ROWS, width // 2), F32),
                pltpu.SemaphoreType.DMA((2,)),
                pltpu.SemaphoreType.DMA((2, n)),
            ]
        return out

    def columns(self, q):
        return pl.ds(q * self.width if isinstance(q, int) else pl.multiple_of(q * self.width, self.width), self.width)

    def rows(self, q, g, pair):
        at = pl.ds(pl.multiple_of(g * 16 + pair * ROWS, ROWS), ROWS)
        return self.acc[at, self.columns(q)]

    def either(self, q, narrow, wide):
        is_wide = False
        for i, w in enumerate(self.wide):
            when(q == w)(functools.partial(wide, i))
            is_wide = (q == w) | is_wide
        if self.wide:
            when(not is_wide if isinstance(is_wide, bool) else jnp.logical_not(is_wide))(narrow)
        else:
            narrow()

    def pair_copy(self, q):
        return remote(
            self.psnd.at[q], self.prcv.at[q], self.sent.at[0], self.came.at[0, q], self.axis.partner()
        )

    def group_copy(self, q, k):
        return remote(
            self.gsnd.at[q, self.axis.groups[k]],
            self.grcv.at[q, k - 1],
            self.sent.at[1],
            self.came.at[1, q],
            self.axis.peers[k],
        )

    def wide_group_copy(self, i, k):
        return remote(
            self.wsnd.at[i, self.axis.groups[k]],
            self.wrcv.at[i, k - 1],
            self.wsent.at[0],
            self.wcame.at[0, i],
            self.axis.peers[k],
        )

    def wide_pair_copy(self, i):
        return remote(
            self.wpsnd.at[i], self.wprcv.at[i], self.wsent.at[1], self.wcame.at[1, i], self.axis.partner()
        )

    def begin(self, q):
        def narrow():
            other = 1 - self.axis.pair
            for g in range(0, GROUP, 2):
                two = jnp.concatenate([self.rows(q, g, other), self.rows(q, g + 1, other)], axis=0)
                self.psnd[q, g * ROWS : (g + 2) * ROWS, :] = two.astype(BF16)
            self.pair_copy(q).start()

        def wide(i):
            def send(k):
                g = self.axis.groups[k]
                both = pl.ds(pl.multiple_of(g * 16, 16), 16)
                self.wsnd[i, g] = self.acc[both, self.columns(q)].astype(BF16)
                if k:
                    self.wide_group_copy(i, k).start()

            each_peer(send)
            send(0)

        self.either(q, narrow, wide)

    def middle(self, q):
        def narrow():
            wait_bytes(self.prcv.at[q], self.came.at[0, q])
            for g in range(0, GROUP, 2):
                came = self.prcv[q, g * ROWS : (g + 2) * ROWS, :].astype(F32)
                for i in range(2):
                    both = self.rows(q, g + i, self.axis.pair) + came[i * ROWS : (i + 1) * ROWS]
                    self.gsnd[q, g + i] = fold(both).astype(BF16)
            each_peer(lambda k: self.group_copy(q, k).start())

        def wide(i):
            wait_bytes(self.wrcv.at[i], self.wcame.at[0, i])
            total = self.wsnd[i, self.axis.group].astype(F32)
            for k in range(GROUP - 1):
                total = total + self.wrcv[i, k].astype(F32)
            even, odd = fold(total[:ROWS]), fold(total[ROWS:])
            is_even = self.axis.pair == 0
            self.wpsnd[i] = jnp.where(is_even, odd, even).astype(BF16)
            self.wsum[i] = jnp.where(is_even, even, odd)
            self.wide_pair_copy(i).start()

        self.either(q, narrow, wide)

    def end(self, q, use):
        def narrow():
            wait_bytes(self.grcv.at[q], self.came.at[1, q])
            total = self.gsnd[q, self.axis.group].astype(F32)
            for k in range(GROUP - 1):
                total = total + self.grcv[q, k].astype(F32)
            use(total)

        def wide(i):
            wait_bytes(self.wprcv.at[i], self.wcame.at[1, i])
            use(self.wsum[i] + self.wprcv[i].astype(F32))

        self.either(q, narrow, wide)

    def drain(self):
        count = self.psnd.shape[0] - len(self.wide)
        wait_bytes(self.psnd.at[pl.ds(0, count)], self.sent.at[0])
        wait_bytes(self.grcv.at[pl.ds(0, count)], self.sent.at[1])
        if self.wide:
            wait_bytes(self.wrcv, self.wsent.at[0])
            wait_bytes(self.wpsnd, self.wsent.at[1])


class Gather:
    def __init__(self, axis, refs):
        self.axis = axis
        self.held, self.sent, self.came = refs

    @staticmethod
    def scratch(chunks, width):
        return [
            pltpu.VMEM((chunks, 2, GROUP, 2 * ROWS, width // 2), BF16),
            pltpu.SemaphoreType.DMA((2,)),
            pltpu.SemaphoreType.DMA((2, chunks)),
        ]

    def pair_copy(self, q):
        mine = self.held.at[q, self.axis.pair]
        return remote(mine, mine, self.sent.at[0], self.came.at[0, q], self.axis.partner())

    def group_copy(self, q, k):
        mine = self.held.at[q, self.axis.pair, self.axis.group]
        return remote(mine, mine, self.sent.at[1], self.came.at[1, q], self.axis.peers[k])

    def send_group(self, q, block):
        self.held[q, self.axis.pair, self.axis.group] = block.astype(BF16)
        each_peer(lambda k: self.group_copy(q, k).start())

    def send_pair(self, q):
        wait_bytes(self.held.at[q, 0, pl.ds(0, GROUP - 1)], self.came.at[1, q])
        self.pair_copy(q).start()

    def wait(self, q):
        wait_bytes(self.held.at[q, 0], self.came.at[0, q])

    def write_rows(self, q, out, start):
        half = self.held.shape[-1]
        for g in range(GROUP):
            even = self.held[q, 0, g].astype(F32)
            odd = self.held[q, 1, g].astype(F32)
            for side in range(2):
                rows = slice(side * ROWS, (side + 1) * ROWS)
                both = jnp.concatenate([even[rows], odd[rows]], axis=0)
                at = start + side * half
                out[g * 16 : g * 16 + 16, at : at + half] = both.astype(BF16)

    def drain(self):
        wait_bytes(self.held.at[:, 0], self.sent.at[0])
        wait_bytes(self.held.at[:, 0, pl.ds(0, GROUP - 1)], self.sent.at[1])


def when(cond):
    if isinstance(cond, (bool, np.bool_)):
        return (lambda f: f()) if cond else (lambda f: None)
    return pl.when(cond)


def staged(steps, stages):
    for t in range(steps):
        for start, run in stages:
            if start <= t < start + CHUNKS:
                run(t - start)


def kernel(amps, integrals, vir, occ, one, two, three, *scratch):
    outs = one, two, three
    scratch = list(scratch)

    def take(n):
        out = scratch[:n]
        del scratch[:n]
        return out

    amps_held, occ_held, block, turned, block_sem, vir_held, vir_sem, den_second, den_first, first, chunk, out_held, out_sem = take(13)
    acc_one, acc_two, acc_three = take(3)
    rows, size = first.shape
    width = size // CHUNKS
    tiles, per_tile = size // TILE, TILE // width
    ab, cd = Axis("ab", "cd"), Axis("cd", "ab")
    scatter_one = Scatter(cd, acc_one, WIDE_ONE, take(13 if WIDE_ONE else 6))
    scatter_two = Scatter(ab, acc_two, (), take(6))
    scatter_three = Scatter(cd, acc_three, WIDE_THREE, take(13 if WIDE_THREE else 6))
    gather_one = Gather(ab, take(3))
    gather_two = Gather(cd, take(3))
    gather_three = Gather(ab, take(3))

    def load(q):
        rows = pl.ds(pl.multiple_of(q * TILE, TILE), TILE)
        return pltpu.make_async_copy(integrals.at[rows, :], block.at[rows, :], block_sem.at[q])

    def load_vir(i, axis):
        rows = size // LANES
        return pltpu.make_async_copy(
            vir.at[pl.ds(pl.multiple_of(axis.index * rows, rows), rows), :], vir_held.at[i], vir_sem.at[i]
        )

    load_amps = pltpu.make_async_copy(amps, amps_held, vir_sem.at[2])
    load_occ = pltpu.make_async_copy(occ, occ_held, vir_sem.at[3])

    barrier = pltpu.get_barrier_semaphore()
    for axis in (ab, cd):
        each_peer(
            lambda k: pl.semaphore_signal(barrier, inc=1, device_id=axis.peers[k], device_id_type=MESH)
        )
        pl.semaphore_signal(barrier, inc=1, device_id=axis.partner(), device_id_type=MESH)
    load_amps.start()
    load_vir(0, ab).start()
    load_vir(1, cd).start()
    load_occ.start()
    for q in range(tiles):
        load(q).start()
    load_amps.wait()
    amp_width = size // AMP_CHUNKS
    pl.semaphore_wait(barrier, 2 * GROUP)
    for i in range(AMP_CHUNKS):
        part = amps_held[:, i * amp_width : (i + 1) * amp_width]
        gather_one.send_group(i, fold(part.astype(F32)))

    load_vir(0, ab).wait()
    load_vir(1, cd).wait()
    load_occ.wait()
    row = lax.broadcasted_iota(jnp.int32, (ROWS, LANES), 0)
    for i, axis, den in ((0, cd, den_second), (1, ab, den_first)):
        levels = jnp.zeros((ROWS, LANES), F32)
        for r in range(ROWS):
            levels = jnp.where(row == r, occ_held[axis.index * ROWS + r], levels)
        for lane_tile in range(size // LANES):
            per_half = width // 2 // LANES
            part = lane_tile // per_half
            q, side, at = part // 2, part % 2, lane_tile % per_half
            den[q, side * ROWS : (side + 1) * ROWS, at * LANES : (at + 1) * LANES] = (
                jnp.broadcast_to(vir_held[i, lane_tile : lane_tile + 1, :], (ROWS, LANES)) - levels
            )
    acc_two[...] = jnp.zeros_like(acc_two)
    acc_three[...] = jnp.zeros_like(acc_three)
    def turn(r):
        load(r).wait()

        def part(c, carry):
            to, at = (pl.ds(pl.multiple_of(i * TILE, TILE), TILE) for i in (r, c))
            turned[at, to] = block[to, at].T
            return carry

        lax.fori_loop(0, tiles, part, 0)

    for r in range(tiles):
        turn(r)
    for i in range(AMP_CHUNKS):
        gather_one.send_pair(i)
    first_tile = jnp.zeros((rows, TILE), F32)
    for i in range(AMP_CHUNKS):
        gather_one.wait(i)
        gather_one.write_rows(i, first, i * amp_width)
        at = slice(i * amp_width, (i + 1) * amp_width)
        first_tile += dot(first[:, at], turned[at, :TILE])
    acc_one[:, :TILE] = first_tile

    def columns(q):
        return pl.ds(q * width if isinstance(q, int) else pl.multiple_of(q * width, width), width)

    def tile(n):
        return pl.ds(n * TILE if isinstance(n, int) else pl.multiple_of(n * TILE, TILE), TILE)

    def product_one(q):
        @when((q % per_tile) == 0)
        def _():
            n = (q // per_tile)

            @when(n > 0)
            def _():
                acc_one[:, tile(n)] = dot(first[...], turned[:, tile(n)])

            for i in range(per_tile):
                scatter_one.begin(q + i)

    def store(i):
        return pltpu.make_async_copy(out_held.at[i], outs[i], out_sem.at[i])

    def finish(scatter, i, den, gather, q):
        def use(total):
            if gather is not None:
                gather.send_group(q, total / den[q])
            out_held[i, :, columns(q)] = unfold(total).astype(BF16)

        scatter.end(q, use)

        @when(q == CHUNKS - 1)
        def _():
            store(i).start()

    def product(gather, scatter, acc, integrals, q):
        gather.wait(q)
        for i in range(per_tile):

            @when((q % per_tile) == i)
            def _():
                gather.write_rows(q, chunk, i * width)

        @when((q % per_tile) == per_tile - 1)
        def _():
            m = (q // per_tile)

            def part(n):
                acc[:, tile(n)] += dot(chunk[...], integrals[tile(m), tile(n)])

                @when(q == CHUNKS - 1)
                def _():
                    for i in range(per_tile):
                        scatter.begin(n * per_tile + i)

            for n in range(tiles):
                part(n)

    s0, s1, s2, s3, s4 = STAGES_ONE
    staged(
        s4 + CHUNKS,
        (
            (s0, product_one),
            (s1, scatter_one.middle),
            (s2, functools.partial(finish, scatter_one, 0, den_second, gather_two)),
            (s3, gather_two.send_pair),
            (s4, functools.partial(product, gather_two, scatter_two, acc_two, block)),
        ),
    )
    s0, s1, s2, s3 = STAGES_TWO
    staged(
        s3 + CHUNKS,
        (
            (s0, scatter_two.middle),
            (s1, functools.partial(finish, scatter_two, 1, den_first, gather_three)),
            (s2, gather_three.send_pair),
            (s3, functools.partial(product, gather_three, scatter_three, acc_three, turned)),
        ),
    )
    s0, s1 = STAGES_THREE
    staged(
        s1 + CHUNKS,
        (
            (s0, scatter_three.middle),
            (s1, functools.partial(finish, scatter_three, 2, None, None)),
        ),
    )

    for part in (gather_one, gather_two, gather_three, scatter_one, scatter_two, scatter_three):
        part.drain()
    for i in range(3):
        store(i).wait()


def hand_on(*refs):
    sources, targets, held, sems = refs[:3], refs[3:6], refs[6], refs[7]
    came = [pltpu.make_async_copy(sources[i], held.at[i], sems.at[i]) for i in range(3)]
    gone = [pltpu.make_async_copy(held.at[i], targets[i], sems.at[i]) for i in range(3)]
    for copy in came:
        copy.start()
    for i in range(3):
        came[i].wait()
        gone[i].start()
    for copy in gone:
        copy.wait()


def per_device(amplitudes, integrals, vir_energy, occ_energy):
    size = integrals.shape[0]
    width = size // CHUNKS
    rows = occ_energy.shape[0]
    hbm = pl.BlockSpec(memory_space=pltpu.HBM)
    out = jax.ShapeDtypeStruct(amplitudes.shape, BF16)
    ladders = pl.pallas_call(
        kernel,
        out_shape=(out, out, out),
        in_specs=[hbm] * 4,
        out_specs=(hbm, hbm, hbm),
        scratch_shapes=[
            pltpu.VMEM(amplitudes.shape, BF16),
            pltpu.SMEM((rows,), F32),
            pltpu.VMEM((size, size), BF16),
            pltpu.VMEM((size, size), BF16),
            pltpu.SemaphoreType.DMA((size // TILE,)),
            pltpu.VMEM((2, size // LANES, LANES), F32),
            pltpu.SemaphoreType.DMA((4,)),
            pltpu.VMEM((CHUNKS, 2 * ROWS, width // 2), F32),
            pltpu.VMEM((CHUNKS, 2 * ROWS, width // 2), F32),
            pltpu.VMEM((rows, size), BF16),
            pltpu.VMEM((rows, TILE), BF16),
            pltpu.VMEM((3,) + amplitudes.shape, BF16),
            pltpu.SemaphoreType.DMA((3,)),
        ]
        + [pltpu.VMEM((rows, size), F32)] * 3
        + Scatter.scratch(CHUNKS, width, WIDE_ONE)
        + Scatter.scratch(CHUNKS, width, ())
        + Scatter.scratch(CHUNKS, width, WIDE_THREE)
        + Gather.scratch(AMP_CHUNKS, size // AMP_CHUNKS)
        + Gather.scratch(CHUNKS, width) * 2,
        compiler_params=pltpu.CompilerParams(
            collective_id=0, has_side_effects=True, vmem_limit_bytes=VMEM_LIMIT
        ),
        cost_estimate=pl.CostEstimate(
            flops=6 * rows * size * size, bytes_accessed=2 * size * size, transcendentals=0
        ),
        name="ladder",
    )(amplitudes, integrals, vir_energy.reshape(-1, LANES), occ_energy)
    return pl.pallas_call(
        hand_on,
        out_shape=(out, out, out),
        in_specs=[hbm] * 3,
        out_specs=(hbm,) * 3,
        scratch_shapes=[pltpu.VMEM((3,) + amplitudes.shape, BF16), pltpu.SemaphoreType.DMA((3,))],
        name="hand_on",
    )(*ladders)


def solution(mesh):
    return jax.shard_map(
        per_device,
        mesh=mesh,
        in_specs=(P("ab", "cd"), P("ab", "cd"), P(), P()),
        out_specs=(P("cd", "ab"), P("ab", "cd"), P("cd", "ab")),
        check_vma=False,
    )
```

```python
import functools

import jax
import jax.numpy as jnp
import numpy as np
from jax import lax
from jax.experimental import pallas as pl
from jax.experimental.pallas import tpu as pltpu
from jax.sharding import PartitionSpec as P

MESH = pl.DeviceIdType.MESH
F32 = jnp.float32
BF16 = jnp.bfloat16

GROUP = 8
LANES = 128
ROWS = 8
CHUNKS = 4
TILE = 512
FAR_FIRST = (4, 3, 5, 2, 6, 1, 7)
VMEM_LIMIT = 60 * 2**20
STAGES_ONE = (0, 4, 7, 10, 13)
STAGES_TWO = (0, 3, 6, 9)
STAGES_THREE = (0, 4)
AMP_CHUNKS = 1
WIDE_ONE = (2,)
WIDE_THREE = (3,)


class Axis:
    def __init__(self, name, other):
        self.name = name
        self.index = lax.axis_index(name)
        self.other = lax.axis_index(other)
        self.group = lax.div(self.index, 2)
        self.pair = lax.rem(self.index, 2)
        self.groups = [lax.rem(self.group + k, GROUP) for k in range(GROUP)]
        self.peers = [self.device(g * 2 + self.pair) for g in self.groups]

    def device(self, index):
        return (index, self.other) if self.name == "ab" else (self.other, index)

    def partner(self):
        return self.device(self.group * 2 + 1 - self.pair)


def remote(src, dst, send, recv, device):
    return pltpu.make_async_remote_copy(
        src_ref=src, dst_ref=dst, send_sem=send, recv_sem=recv, device_id=device, device_id_type=MESH
    )


def each_peer(body):
    for k in FAR_FIRST:
        body(k)


def dot(left, right):
    return jnp.dot(left, right, preferred_element_type=F32)


def wait_bytes(ref, sem):
    pltpu.make_async_copy(ref, ref, sem).wait()


def fold(block):
    half = block.shape[1] // 2
    return jnp.concatenate([block[:, :half], block[:, half:]], axis=0)


def unfold(block):
    return jnp.concatenate([block[:ROWS], block[ROWS:]], axis=1)


class Scatter:
    def __init__(self, axis, acc, wide, refs):
        self.axis, self.acc, self.wide = axis, acc, wide
        self.psnd, self.prcv, self.gsnd, self.grcv, self.sent, self.came = refs[:6]
        if wide:
            self.wsnd, self.wrcv, self.wpsnd, self.wprcv, self.wsum, self.wsent, self.wcame = refs[6:]
        self.width = self.psnd.shape[-1]

    @staticmethod
    def scratch(chunks, width, wide):
        out = [
            pltpu.VMEM((chunks, GROUP * ROWS, width), BF16),
            pltpu.VMEM((chunks, GROUP * ROWS, width), BF16),
            pltpu.VMEM((chunks, GROUP, 2 * ROWS, width // 2), BF16),
            pltpu.VMEM((chunks, GROUP - 1, 2 * ROWS, width // 2), BF16),
            pltpu.SemaphoreType.DMA((2,)),
            pltpu.SemaphoreType.DMA((2, chunks)),
        ]
        if wide:
            n = len(wide)
            out += [
                pltpu.VMEM((n, GROUP, 2 * ROWS, width), BF16),
                pltpu.VMEM((n, GROUP - 1, 2 * ROWS, width), BF16),
                pltpu.VMEM((n, 2 * ROWS, width // 2), BF16),
                pltpu.VMEM((n, 2 * ROWS, width // 2), BF16),
                pltpu.VMEM((n, 2 * ROWS, width // 2), F32),
                pltpu.SemaphoreType.DMA((2,)),
                pltpu.SemaphoreType.DMA((2, n)),
            ]
        return out

    def columns(self, q):
        return pl.ds(q * self.width if isinstance(q, int) else pl.multiple_of(q * self.width, self.width), self.width)

    def rows(self, q, g, pair):
        at = pl.ds(pl.multiple_of(g * 16 + pair * ROWS, ROWS), ROWS)
        return self.acc[at, self.columns(q)]

    def either(self, q, narrow, wide):
        is_wide = False
        for i, w in enumerate(self.wide):
            when(q == w)(functools.partial(wide, i))
            is_wide = (q == w) | is_wide
        if self.wide:
            when(not is_wide if isinstance(is_wide, bool) else jnp.logical_not(is_wide))(narrow)
        else:
            narrow()

    def pair_copy(self, q):
        return remote(
            self.psnd.at[q], self.prcv.at[q], self.sent.at[0], self.came.at[0, q], self.axis.partner()
        )

    def group_copy(self, q, k):
        return remote(
            self.gsnd.at[q, self.axis.groups[k]],
            self.grcv.at[q, k - 1],
            self.sent.at[1],
            self.came.at[1, q],
            self.axis.peers[k],
        )

    def wide_group_copy(self, i, k):
        return remote(
            self.wsnd.at[i, self.axis.groups[k]],
            self.wrcv.at[i, k - 1],
            self.wsent.at[0],
            self.wcame.at[0, i],
            self.axis.peers[k],
        )

    def wide_pair_copy(self, i):
        return remote(
            self.wpsnd.at[i], self.wprcv.at[i], self.wsent.at[1], self.wcame.at[1, i], self.axis.partner()
        )

    def begin(self, q):
        def narrow():
            other = 1 - self.axis.pair
            for g in range(0, GROUP, 2):
                two = jnp.concatenate([self.rows(q, g, other), self.rows(q, g + 1, other)], axis=0)
                self.psnd[q, g * ROWS : (g + 2) * ROWS, :] = two.astype(BF16)
            self.pair_copy(q).start()

        def wide(i):
            def send(k):
                g = self.axis.groups[k]
                both = pl.ds(pl.multiple_of(g * 16, 16), 16)
                self.wsnd[i, g] = self.acc[both, self.columns(q)].astype(BF16)
                if k:
                    self.wide_group_copy(i, k).start()

            each_peer(send)
            send(0)

        self.either(q, narrow, wide)

    def middle(self, q):
        def narrow():
            wait_bytes(self.prcv.at[q], self.came.at[0, q])
            for g in range(0, GROUP, 2):
                came = self.prcv[q, g * ROWS : (g + 2) * ROWS, :].astype(F32)
                for i in range(2):
                    both = self.rows(q, g + i, self.axis.pair) + came[i * ROWS : (i + 1) * ROWS]
                    self.gsnd[q, g + i] = fold(both).astype(BF16)
            each_peer(lambda k: self.group_copy(q, k).start())

        def wide(i):
            wait_bytes(self.wrcv.at[i], self.wcame.at[0, i])
            total = self.wsnd[i, self.axis.group].astype(F32)
            for k in range(GROUP - 1):
                total = total + self.wrcv[i, k].astype(F32)
            even, odd = fold(total[:ROWS]), fold(total[ROWS:])
            is_even = self.axis.pair == 0
            self.wpsnd[i] = jnp.where(is_even, odd, even).astype(BF16)
            self.wsum[i] = jnp.where(is_even, even, odd)
            self.wide_pair_copy(i).start()

        self.either(q, narrow, wide)

    def end(self, q, use):
        def narrow():
            wait_bytes(self.grcv.at[q], self.came.at[1, q])
            total = self.gsnd[q, self.axis.group].astype(F32)
            for k in range(GROUP - 1):
                total = total + self.grcv[q, k].astype(F32)
            use(total)

        def wide(i):
            wait_bytes(self.wprcv.at[i], self.wcame.at[1, i])
            use(self.wsum[i] + self.wprcv[i].astype(F32))

        self.either(q, narrow, wide)

    def drain(self):
        count = self.psnd.shape[0] - len(self.wide)
        wait_bytes(self.psnd.at[pl.ds(0, count)], self.sent.at[0])
        wait_bytes(self.grcv.at[pl.ds(0, count)], self.sent.at[1])
        if self.wide:
            wait_bytes(self.wrcv, self.wsent.at[0])
            wait_bytes(self.wpsnd, self.wsent.at[1])


class Gather:
    def __init__(self, axis, refs):
        self.axis = axis
        self.held, self.sent, self.came = refs

    @staticmethod
    def scratch(chunks, width):
        return [
            pltpu.VMEM((chunks, 2, GROUP, 2 * ROWS, width // 2), BF16),
            pltpu.SemaphoreType.DMA((2,)),
            pltpu.SemaphoreType.DMA((2, chunks)),
        ]

    def pair_copy(self, q):
        mine = self.held.at[q, self.axis.pair]
        return remote(mine, mine, self.sent.at[0], self.came.at[0, q], self.axis.partner())

    def group_copy(self, q, k):
        mine = self.held.at[q, self.axis.pair, self.axis.group]
        return remote(mine, mine, self.sent.at[1], self.came.at[1, q], self.axis.peers[k])

    def send_group(self, q, block):
        self.held[q, self.axis.pair, self.axis.group] = block.astype(BF16)
        each_peer(lambda k: self.group_copy(q, k).start())

    def send_pair(self, q):
        wait_bytes(self.held.at[q, 0, pl.ds(0, GROUP - 1)], self.came.at[1, q])
        self.pair_copy(q).start()

    def wait(self, q):
        wait_bytes(self.held.at[q, 0], self.came.at[0, q])

    def write_rows(self, q, out, start):
        half = self.held.shape[-1]
        for g in range(GROUP):
            even = self.held[q, 0, g].astype(F32)
            odd = self.held[q, 1, g].astype(F32)
            for side in range(2):
                rows = slice(side * ROWS, (side + 1) * ROWS)
                both = jnp.concatenate([even[rows], odd[rows]], axis=0)
                at = start + side * half
                out[g * 16 : g * 16 + 16, at : at + half] = both.astype(BF16)

    def drain(self):
        wait_bytes(self.held.at[:, 0], self.sent.at[0])
        wait_bytes(self.held.at[:, 0, pl.ds(0, GROUP - 1)], self.sent.at[1])


def when(cond):
    if isinstance(cond, (bool, np.bool_)):
        return (lambda f: f()) if cond else (lambda f: None)
    return pl.when(cond)


def staged(steps, stages):
    for t in range(steps):
        for start, run in stages:
            if start <= t < start + CHUNKS:
                run(t - start)


def kernel(amps, integrals, vir, occ, one, two, three, *scratch):
    outs = one, two, three
    scratch = list(scratch)

    def take(n):
        out = scratch[:n]
        del scratch[:n]
        return out

    amps_held, occ_held, block, turned, block_sem, vir_held, vir_sem, den_second, den_first, first, chunk, out_held, out_sem = take(13)
    acc_one, acc_two, acc_three = take(3)
    rows, size = first.shape
    width = size // CHUNKS
    tiles, per_tile = size // TILE, TILE // width
    ab, cd = Axis("ab", "cd"), Axis("cd", "ab")
    scatter_one = Scatter(cd, acc_one, WIDE_ONE, take(13 if WIDE_ONE else 6))
    scatter_two = Scatter(ab, acc_two, (), take(6))
    scatter_three = Scatter(cd, acc_three, WIDE_THREE, take(13 if WIDE_THREE else 6))
    gather_one = Gather(ab, take(3))
    gather_two = Gather(cd, take(3))
    gather_three = Gather(ab, take(3))

    def load(q):
        rows = pl.ds(pl.multiple_of(q * TILE, TILE), TILE)
        return pltpu.make_async_copy(integrals.at[rows, :], block.at[rows, :], block_sem.at[q])

    def load_vir(i, axis):
        rows = size // LANES
        return pltpu.make_async_copy(
            vir.at[pl.ds(pl.multiple_of(axis.index * rows, rows), rows), :], vir_held.at[i], vir_sem.at[i]
        )

    load_amps = pltpu.make_async_copy(amps, amps_held, vir_sem.at[2])
    load_occ = pltpu.make_async_copy(occ, occ_held, vir_sem.at[3])

    barrier = pltpu.get_barrier_semaphore()
    for axis in (ab, cd):
        each_peer(
            lambda k: pl.semaphore_signal(barrier, inc=1, device_id=axis.peers[k], device_id_type=MESH)
        )
        pl.semaphore_signal(barrier, inc=1, device_id=axis.partner(), device_id_type=MESH)
    load_amps.start()
    load_vir(0, ab).start()
    load_vir(1, cd).start()
    load_occ.start()
    for q in range(tiles):
        load(q).start()
    load_amps.wait()
    amp_width = size // AMP_CHUNKS
    pl.semaphore_wait(barrier, 2 * GROUP)
    for i in range(AMP_CHUNKS):
        part = amps_held[:, i * amp_width : (i + 1) * amp_width]
        gather_one.send_group(i, fold(part.astype(F32)))

    load_vir(0, ab).wait()
    load_vir(1, cd).wait()
    load_occ.wait()
    row = lax.broadcasted_iota(jnp.int32, (ROWS, LANES), 0)
    for i, axis, den in ((0, cd, den_second), (1, ab, den_first)):
        levels = jnp.zeros((ROWS, LANES), F32)
        for r in range(ROWS):
            levels = jnp.where(row == r, occ_held[axis.index * ROWS + r], levels)
        for lane_tile in range(size // LANES):
            per_half = width // 2 // LANES
            part = lane_tile // per_half
            q, side, at = part // 2, part % 2, lane_tile % per_half
            den[q, side * ROWS : (side + 1) * ROWS, at * LANES : (at + 1) * LANES] = (
                jnp.broadcast_to(vir_held[i, lane_tile : lane_tile + 1, :], (ROWS, LANES)) - levels
            )
    def turn(r):
        load(r).wait()

        def part(c, carry):
            to, at = (pl.ds(pl.multiple_of(i * TILE, TILE), TILE) for i in (r, c))
            turned[at, to] = block[to, at].T
            return carry

        lax.fori_loop(0, tiles, part, 0)

    for r in range(tiles):
        turn(r)
    for i in range(AMP_CHUNKS):
        gather_one.send_pair(i)
    first_tile = jnp.zeros((rows, TILE), F32)
    for i in range(AMP_CHUNKS):
        gather_one.wait(i)
        gather_one.write_rows(i, first, i * amp_width)
        at = slice(i * amp_width, (i + 1) * amp_width)
        first_tile += dot(first[:, at], turned[at, :TILE])
    acc_one[:, :TILE] = first_tile

    def columns(q):
        return pl.ds(q * width if isinstance(q, int) else pl.multiple_of(q * width, width), width)

    def tile(n):
        return pl.ds(n * TILE if isinstance(n, int) else pl.multiple_of(n * TILE, TILE), TILE)

    def product_one(q):
        @when((q % per_tile) == 0)
        def _():
            n = (q // per_tile)

            @when(n > 0)
            def _():
                acc_one[:, tile(n)] = dot(first[...], turned[:, tile(n)])

            for i in range(per_tile):
                scatter_one.begin(q + i)

    def store(i):
        return pltpu.make_async_copy(out_held.at[i], outs[i], out_sem.at[i])

    def finish(scatter, i, den, gather, q):
        def use(total):
            if gather is not None:
                gather.send_group(q, total / den[q])
            out_held[i, :, columns(q)] = unfold(total).astype(BF16)

        scatter.end(q, use)

        @when(q == CHUNKS - 1)
        def _():
            store(i).start()

    def product(gather, scatter, acc, integrals, q):
        gather.wait(q)
        for i in range(per_tile):

            @when((q % per_tile) == i)
            def _():
                gather.write_rows(q, chunk, i * width)

        @when((q % per_tile) == per_tile - 1)
        def _():
            m = (q // per_tile)

            def part(n):
                term = dot(chunk[...], integrals[tile(m), tile(n)])
                acc[:, tile(n)] = term if m == 0 else acc[:, tile(n)] + term

                @when(q == CHUNKS - 1)
                def _():
                    for i in range(per_tile):
                        scatter.begin(n * per_tile + i)

            for n in range(tiles):
                part(n)

    s0, s1, s2, s3, s4 = STAGES_ONE
    staged(
        s4 + CHUNKS,
        (
            (s0, product_one),
            (s1, scatter_one.middle),
            (s2, functools.partial(finish, scatter_one, 0, den_second, gather_two)),
            (s3, gather_two.send_pair),
            (s4, functools.partial(product, gather_two, scatter_two, acc_two, block)),
        ),
    )
    s0, s1, s2, s3 = STAGES_TWO
    staged(
        s3 + CHUNKS,
        (
            (s0, scatter_two.middle),
            (s1, functools.partial(finish, scatter_two, 1, den_first, gather_three)),
            (s2, gather_three.send_pair),
            (s3, functools.partial(product, gather_three, scatter_three, acc_three, turned)),
        ),
    )
    s0, s1 = STAGES_THREE
    staged(
        s1 + CHUNKS,
        (
            (s0, scatter_three.middle),
            (s1, functools.partial(finish, scatter_three, 2, None, None)),
        ),
    )

    for part in (gather_one, gather_two, gather_three, scatter_one, scatter_two, scatter_three):
        part.drain()
    for i in range(3):
        store(i).wait()


def hand_on(*refs):
    sources, targets, held, sems = refs[:3], refs[3:6], refs[6], refs[7]
    came = [pltpu.make_async_copy(sources[i], held.at[i], sems.at[i]) for i in range(3)]
    gone = [pltpu.make_async_copy(held.at[i], targets[i], sems.at[i]) for i in range(3)]
    for copy in came:
        copy.start()
    for i in range(3):
        came[i].wait()
        gone[i].start()
    for copy in gone:
        copy.wait()


def per_device(amplitudes, integrals, vir_energy, occ_energy):
    size = integrals.shape[0]
    width = size // CHUNKS
    rows = occ_energy.shape[0]
    hbm = pl.BlockSpec(memory_space=pltpu.HBM)
    out = jax.ShapeDtypeStruct(amplitudes.shape, BF16)
    ladders = pl.pallas_call(
        kernel,
        out_shape=(out, out, out),
        in_specs=[hbm] * 4,
        out_specs=(hbm, hbm, hbm),
        scratch_shapes=[
            pltpu.VMEM(amplitudes.shape, BF16),
            pltpu.SMEM((rows,), F32),
            pltpu.VMEM((size, size), BF16),
            pltpu.VMEM((size, size), BF16),
            pltpu.SemaphoreType.DMA((size // TILE,)),
            pltpu.VMEM((2, size // LANES, LANES), F32),
            pltpu.SemaphoreType.DMA((4,)),
            pltpu.VMEM((CHUNKS, 2 * ROWS, width // 2), F32),
            pltpu.VMEM((CHUNKS, 2 * ROWS, width // 2), F32),
            pltpu.VMEM((rows, size), BF16),
            pltpu.VMEM((rows, TILE), BF16),
            pltpu.VMEM((3,) + amplitudes.shape, BF16),
            pltpu.SemaphoreType.DMA((3,)),
        ]
        + [pltpu.VMEM((rows, size), F32)] * 3
        + Scatter.scratch(CHUNKS, width, WIDE_ONE)
        + Scatter.scratch(CHUNKS, width, ())
        + Scatter.scratch(CHUNKS, width, WIDE_THREE)
        + Gather.scratch(AMP_CHUNKS, size // AMP_CHUNKS)
        + Gather.scratch(CHUNKS, width) * 2,
        compiler_params=pltpu.CompilerParams(
            collective_id=0, has_side_effects=True, vmem_limit_bytes=VMEM_LIMIT
        ),
        cost_estimate=pl.CostEstimate(
            flops=6 * rows * size * size, bytes_accessed=2 * size * size, transcendentals=0
        ),
        name="ladder",
    )(amplitudes, integrals, vir_energy.reshape(-1, LANES), occ_energy)
    return pl.pallas_call(
        hand_on,
        out_shape=(out, out, out),
        in_specs=[hbm] * 3,
        out_specs=(hbm,) * 3,
        scratch_shapes=[pltpu.VMEM((3,) + amplitudes.shape, BF16), pltpu.SemaphoreType.DMA((3,))],
        name="hand_on",
    )(*ladders)


def solution(mesh):
    return jax.shard_map(
        per_device,
        mesh=mesh,
        in_specs=(P("ab", "cd"), P("ab", "cd"), P(), P()),
        out_specs=(P("cd", "ab"), P("ab", "cd"), P("cd", "ab")),
        check_vma=False,
    )
```
